32 devices in a mesh: groups: 2 (over y), aux: 4 (over z), ao: 2 (over x), occ: 2 (over core).
Axes of the slice: x: 2, y: 2, z: 4, core: 2. Of those that a mesh axis runs over, the one named last changes fastest.
Arguments:
- integrals: bfloat16 [16, 1024, 1536], P(('groups', 'aux'), 'ao'), parts along dimension 0, may hold values from -0.15625 to 0.15625
- coefficients: bfloat16 [2048, 2048], P(('groups', 'ao'), 'occ'), parts along dimension 0, may hold values from -6 to 6
- significant: int32 [16, 16], P(('groups', 'ao'), 'occ'), parts along dimension 0, may hold values 0 or 1
- domain: int32 [8, 16], P(('groups', 'aux'), 'occ'), parts along dimension 0, may hold values from 1 to 2
Outputs:
- exchange: float32 [2048, 1536], P(('groups', 'ao'), ('aux', 'occ')), parts along dimension 0
The draws below stay inside these ranges and needn't reach their ends.
There are 2 independent parts, one for each index of `groups`. The reference program is written for one: setup_inputs(seed, part) draws one part's arguments, and reference() takes and returns one part's arrays. A program takes and returns all parts, laid end to end along the dimension named above; each array names one. Nothing has to cross between parts.
All inputs are finite; a program needn't handle non-finite values. No bound on the sum of `significant` on one device may be relied on, other than what follows from the above.
Results may differ from the reference program's by a relative error of at most 0.0011.
Values may be sent and summed in bfloat16 or wider, within the bound.
A program may use at most 64 MiB of HBM per device.

```python
import math
import jax
import jax.numpy as jnp

TILE = 128
HW = 512
PS = 2
AO_DEV = 512
W = 1536
NAUX = 8
NAO = 1024
NOCC = 2048
NAOB = 8
NOB = 16
N_AUX = 4
N_AO = 2


def with_ends(values, rng, least, top_value):
    shape = values.shape
    index_at = [jax.random.randint(jax.random.fold_in(rng, axis), (), 0, shape[axis]) for axis in range(len(shape))]
    values = values.at[tuple(index_at)].set(least)
    longest = shape.index(max(shape))
    index_at[longest] = (index_at[longest] + 1) % shape[longest]
    return values.at[tuple(index_at)].set(top_value)


def steps_of(rng, extent, cuts, smallest, top_value):
    loudness = 1.0
    for axis_at, parts in cuts:
        draws = jax.random.uniform(jax.random.fold_in(jax.random.fold_in(rng, 6), axis_at), (parts,), jnp.float32, smallest / len(cuts), top_value / len(cuts))
        loudness = loudness * jnp.repeat(jnp.exp(draws), extent[axis_at] // parts).reshape((-1,) + (1,) * (len(extent) - 1 - axis_at))
    return loudness


def noise(stream_key, dims, scale, limit, cuts=(), kind=jnp.bfloat16):
    level = steps_of(stream_key, dims, cuts, -0.22, 0.18) if cuts else 1.0
    array = jax.random.normal(stream_key, dims, jnp.float32) * scale * level
    return jnp.minimum(jnp.maximum(array, -limit), limit).astype(kind)


def setup_inputs(seed: int = 0, part: int = 0) -> dict:
    seeds = jax.random.split(jax.random.key(seed), 5)
    part_keys = jax.random.split(jax.random.fold_in(seeds[4], part), 5)
    return {
        "integrals": noise(part_keys[0], (NAUX, NAO, W), W ** -0.5, 0.15625, ((0, 4), (1, 2))),
        "coefficients": noise(part_keys[1], (NAO, NOCC), 1.0, 6.0, ((0, 2), (1, 2))),
        "significant": with_ends((jax.random.randint(part_keys[2], (NAOB, NOB), 0, 3) < 2).astype(jnp.int32), jax.random.fold_in(part_keys[2], 1), 0, 1),
        "domain": with_ends(jax.random.randint(part_keys[3], (N_AUX, NOB), 1, PS + 1), jax.random.fold_in(part_keys[3], 1), 1, PS).astype(jnp.int32),
    }


def reference(integrals, coefficients, significant, domain):
    expanded = jnp.repeat(jnp.repeat(significant, TILE, 0), TILE, 1)
    masked = coefficients * expanded.astype(jnp.bfloat16)
    padded = jnp.pad(masked, ((HW, HW), (0, 0)))
    aux_place = jnp.arange(NAUX, dtype=jnp.int32) % PS
    limits = jnp.repeat(jnp.repeat(domain, PS, 0), TILE, 1)
    retain = (aux_place[:, None] < limits).astype(jnp.float32)
    pieces = []
    for device_row in range(N_AO):
        window = padded[device_row * AO_DEV:device_row * AO_DEV + W].astype(jnp.float32)
        own_rows = integrals[:, device_row * AO_DEV:(device_row + 1) * AO_DEV, :].astype(jnp.float32)
        product = jnp.einsum('pmc,ci->pmi', own_rows, window)
        pieces.append((product * retain[:, None, :]).astype(jnp.bfloat16))
    half_form = jnp.concatenate(pieces, 1)
    half_padded = jnp.pad(half_form, ((0, 0), (HW, HW), (0, 0)))
    factor = 1.0 / math.sqrt(NAUX * NOCC)
    results = []
    for device_row in range(N_AO):
        own_block = half_form[:, device_row * AO_DEV:(device_row + 1) * AO_DEV].astype(jnp.float32)
        nearby = half_padded[:, device_row * AO_DEV:device_row * AO_DEV + W].astype(jnp.float32)
        results.append(jnp.einsum('pmi,pci->mc', own_block, nearby) * factor)
    return jnp.concatenate(results, 0)
```

```python
import functools
import math

import jax
import jax.numpy as jnp
from jax import lax
from jax.experimental import pallas as pl
from jax.experimental.pallas import tpu as pltpu
from jax.sharding import PartitionSpec as P

TILE = 128
MESH = pl.DeviceIdType.MESH
F32 = jnp.float32
BF16 = jnp.bfloat16
C_CHUNKS = 4
NB = 4


def with_halo(block, sides, width):
    for axis, dim in sides:
        count = lax.axis_size(axis)
        forward = [(i, i + 1) for i in range(count - 1)]
        backward = [(target, source) for source, target in forward]
        low = lax.ppermute(
            lax.slice_in_dim(block, block.shape[dim] - width, None, axis=dim), axis, forward
        )
        high = lax.ppermute(lax.slice_in_dim(block, 0, width, axis=dim), axis, backward)
        block = jnp.concatenate([low, block, high], axis=dim)
    return block


def per_device(integrals, coefficients, significant, domain):
    slab_count = integrals.shape[0]
    row_count = integrals.shape[1]
    band_width = integrals.shape[2]
    occ_count = coefficients.shape[1]
    reach = (band_width - row_count) // 2
    expanded = jnp.repeat(jnp.repeat(significant, TILE, 0), TILE, 1)
    masked = coefficients * expanded.astype(jnp.bfloat16)
    window = with_halo(masked, (("ao", 0),), reach)
    flattened = integrals.reshape(slab_count * row_count, band_width)
    product = jnp.dot(flattened, window, preferred_element_type=jnp.float32)
    product = product.reshape(slab_count, row_count, occ_count)
    limits = jnp.repeat(domain[0], TILE)
    aux_place = jnp.arange(slab_count, dtype=jnp.int32)
    retain = (aux_place[:, None] < limits[None, :]).astype(jnp.float32)
    half_form = (product * retain[:, None, :]).astype(jnp.bfloat16)
    nearby = with_halo(half_form, (("ao", 1),), reach)
    aux_devices = lax.axis_size("aux")
    occ_devices = lax.axis_size("occ")
    factor = 1.0 / math.sqrt(slab_count * aux_devices * occ_count * occ_devices)
    exchange_term = (
        lax.dot_general(
            half_form, nearby, (((0, 2), (0, 2)), ((), ())), preferred_element_type=jnp.float32
        )
        * factor
    )
    return lax.psum_scatter(exchange_term, ("aux", "occ"), scatter_dimension=1, tiled=True)


def dot_nt(a, b):
    return lax.dot_general(a, b, (((1,), (1,)), ((), ())), preferred_element_type=F32)


def aligned(value, unit):
    return pl.multiple_of(value, unit)


def pair_kernel(
    naux, rows, occ, factor,
    sig_ref, dom_ref, int_ref, coef_ref, out_ref,
    craw, cw, iw, inb, acc, h, hn, kt, kc, rup, rdn, keep,
    load_sem, c_send, c_recv, f_send, f_recv, i_send, i_recv, g_send, g_recv,
    k_send, k_recv, up_send, up_recv, dn_send, dn_recv,
):
    z = lax.axis_index("aux")
    x = lax.axis_index("ao")
    o = lax.axis_index("occ")
    par = lax.rem(z, 2)
    partner = z + 1 - 2 * par
    unit = kt.shape[1]
    per_dev = out_ref.shape[0] // unit
    side = rows // unit
    crow = rows // 2 // C_CHUNKS
    irow = rows // NB // 2

    load_c = pltpu.make_async_copy(coef_ref, craw, load_sem.at[0])
    load_c.start()
    loads = []
    for p in range(2):
        load = pltpu.make_async_copy(
            int_ref.at[p, :, pl.ds(aligned((1 - x) * rows, rows), 2 * rows)],
            iw.at[pl.ds(p * rows, rows)],
            load_sem.at[1 + p],
        )
        load.start()
        loads.append(load)

    barrier = pltpu.get_barrier_semaphore()
    pl.semaphore_signal(barrier, inc=1, device_id={"ao": 1 - x}, device_id_type=MESH)
    pl.semaphore_signal(barrier, inc=1, device_id={"occ": 1 - o}, device_id_type=MESH)

    @pl.when(z > 0)
    def _():
        pl.semaphore_signal(barrier, inc=1, device_id={"aux": z - 1}, device_id_type=MESH)

    @pl.when(z < naux - 1)
    def _():
        pl.semaphore_signal(barrier, inc=1, device_id={"aux": z + 1}, device_id_type=MESH)

    block_of = lax.broadcasted_iota(jnp.int32, (1, occ), 1) // TILE

    def expand(ref, row):
        line = jnp.zeros((1, occ), F32)
        for j in range(occ // TILE):
            line = jnp.where(block_of == j, ref[row, j].astype(F32), line)
        return line

    limits = expand(dom_ref, 0)
    for p in range(2):
        keep[p : p + 1, :] = jnp.where(limits > float(p), 1.0, 0.0)
    load_c.wait()
    for b in range(rows // TILE):
        mask = expand(sig_ref, b).astype(BF16)
        cw[pl.ds(aligned(x * rows + b * TILE, TILE), TILE), :] = (
            craw[b * TILE : (b + 1) * TILE, :] * mask
        )

    @pl.when((z > 0) & (z < naux - 1))
    def _():
        pl.semaphore_wait(barrier, 4)

    @pl.when((z == 0) | (z == naux - 1))
    def _():
        pl.semaphore_wait(barrier, 3)

    def c_copy(k, owner, half, send, recv, target):
        part = cw.at[pl.ds(aligned(owner * rows + half * (rows // 2) + k * crow, crow), crow)]
        return pltpu.make_async_remote_copy(
            src_ref=part, dst_ref=part, send_sem=send.at[k], recv_sem=recv.at[k],
            device_id=target, device_id_type=MESH,
        )

    def c_across(k):
        return c_copy(k, x, par, c_send, c_recv, {"ao": 1 - x})

    def c_arrival(k):
        return c_copy(k, 1 - x, par, c_send, c_recv, {"ao": 1 - x})

    def c_forward(k):
        return c_copy(k, 1 - x, par, f_send, f_recv, {"aux": partner})

    def c_forwarded(k):
        return c_copy(k, 1 - x, 1 - par, f_send, f_recv, {"aux": partner})

    for k in range(C_CHUNKS):
        c_across(k).start()

    def order(step):
        return step + (NB - 1 - 2 * step) * (1 - x)

    def i_across(step, p):
        j = order_peer(step)
        return pltpu.make_async_remote_copy(
            src_ref=iw.at[pl.ds(aligned(p * rows + j * 2 * irow + o * irow, irow), irow)],
            dst_ref=inb.at[pl.ds(aligned(step * 4 * irow + p * 2 * irow + o * irow, irow), irow)],
            send_sem=i_send.at[step, p], recv_sem=i_recv.at[step, p],
            device_id={"ao": 1 - x}, device_id_type=MESH,
        )

    def order_peer(step):
        return step + (NB - 1 - 2 * step) * x

    def i_core(step, p, core):
        part = inb.at[pl.ds(aligned(step * 4 * irow + p * 2 * irow + core * irow, irow), irow)]
        return pltpu.make_async_remote_copy(
            src_ref=part, dst_ref=part, send_sem=g_send.at[step, p], recv_sem=g_recv.at[step, p],
            device_id={"occ": 1 - o}, device_id_type=MESH,
        )

    for load in loads:
        load.wait()

    width = 256
    own_rows = pl.ds(aligned(x * rows, rows), rows)
    far_rows = pl.ds(aligned((1 - x) * rows, rows), rows)

    def own_tile(t, carry):
        cols = pl.ds(aligned(t * width, width), width)
        acc[:, cols] = jnp.dot(iw[:, own_rows], cw[own_rows, cols], preferred_element_type=F32)
        return carry

    lax.fori_loop(0, occ // width, own_tile, 0)

    for k in range(C_CHUNKS):
        c_arrival(k).wait_recv()
        c_forward(k).start()
    for k in range(C_CHUNKS):
        c_across(k).wait_send()
    for step in range(NB):
        for p in range(2):
            i_across(step, p).start()
    for k in range(C_CHUNKS):
        c_forwarded(k).wait_recv()

    def far_tile(t, carry):
        cols = pl.ds(aligned(t * width, width), width)
        total = acc[:, cols] + jnp.dot(
            iw[:, far_rows], cw[far_rows, cols], preferred_element_type=F32
        )
        for p in range(2):
            h[p * rows : (p + 1) * rows, cols] = (
                total[p * rows : (p + 1) * rows] * keep[p : p + 1, cols]
            ).astype(BF16)
        return carry

    lax.fori_loop(0, occ // width, far_tile, 0)

    def core_copy(idx):
        return pltpu.make_async_remote_copy(
            src_ref=kt.at[idx], dst_ref=kc.at[idx], send_sem=k_send.at[idx],
            recv_sem=k_recv.at[idx], device_id={"occ": 1 - o}, device_id_type=MESH,
        )

    def up_copy(idx):
        return pltpu.make_async_remote_copy(
            src_ref=kt.at[idx], dst_ref=rup.at[idx], send_sem=up_send.at[idx],
            recv_sem=up_recv.at[idx], device_id={"aux": z + 1}, device_id_type=MESH,
        )

    def down_copy(idx):
        return pltpu.make_async_remote_copy(
            src_ref=kt.at[idx], dst_ref=rdn.at[idx], send_sem=dn_send.at[idx],
            recv_sem=dn_recv.at[idx], device_id={"aux": z - 1}, device_id_type=MESH,
        )

    def place(idx):
        owner = idx // per_dev
        return owner // 2, lax.rem(owner, 2), lax.rem(idx, per_dev)

    def share(idx):
        _, ot, _ = place(idx)

        @pl.when(ot != o)
        def _():
            core_copy(idx).start()

    def chain(idx):
        zt, ot, s = place(idx)

        @pl.when(ot == o)
        def _():
            core_copy(idx).wait_recv()
            kt[idx] = kt[idx] + kc[idx]

            @pl.when((z > 0) & (z <= zt))
            def _():
                up_copy(idx).wait_recv()
                kt[idx] = kt[idx] + rup[idx]

            @pl.when((z < naux - 1) & (z >= zt))
            def _():
                down_copy(idx).wait_recv()
                kt[idx] = kt[idx] + rdn[idx]

            @pl.when(z < zt)
            def _():
                up_copy(idx).start()

            @pl.when(z > zt)
            def _():
                down_copy(idx).start()

            @pl.when(z == zt)
            def _():
                out_ref[pl.ds(aligned(s * unit, unit), unit), :] = kt[idx] * factor

    def finish(idx):
        zt, ot, _ = place(idx)

        @pl.when(ot != o)
        def _():
            core_copy(idx).wait_send()

        @pl.when((ot == o) & (z < zt))
        def _():
            up_copy(idx).wait_send()

        @pl.when((ot == o) & (z > zt))
        def _():
            down_copy(idx).wait_send()

    def each(first, count, body):
        def step(n, carry):
            body(first + n)
            return carry

        lax.fori_loop(0, count, step, 0)

    out_ref[...] = jnp.zeros_like(out_ref)

    def own_block(t, carry):
        base = aligned(t * 2 * unit, 2 * unit)
        value = dot_nt(h[pl.ds(base, 2 * unit), :], h[0:rows, :]) + dot_nt(
            h[pl.ds(aligned(rows + base, 2 * unit), 2 * unit), :], h[rows : 2 * rows, :]
        )
        kt[side + 2 * t] = value[:unit]
        kt[side + 2 * t + 1] = value[unit:]
        share(side + 2 * t)
        share(side + 2 * t + 1)
        return carry

    lax.fori_loop(0, side // 2, own_block, 0)

    far_first = 2 * side * (1 - x)
    per_step = side // NB
    for step in range(NB):
        for p in range(2):
            i_across(step, p).wait_recv()
            i_core(step, p, o).start()
        if step < 2:
            each(side + step * (side // 2), side // 2, chain)
        else:
            each(far_first + per_step * order(step - 2), per_step, chain)
        for p in range(2):
            i_core(step, p, 1 - o).wait_recv()
        base = step * 4 * irow

        def near_tile(t, carry):
            cols = pl.ds(aligned(t * width, width), width)
            total = jnp.dot(
                inb[base : base + 4 * irow, :], cw[:, cols], preferred_element_type=F32
            )
            for p in range(2):
                hn[p * 2 * irow : (p + 1) * 2 * irow, cols] = (
                    total[p * 2 * irow : (p + 1) * 2 * irow] * keep[p : p + 1, cols]
                ).astype(BF16)
            return carry

        lax.fori_loop(0, occ // width, near_tile, 0)
        value = dot_nt(hn[0 : 2 * irow, :], h[0:rows, :]) + dot_nt(
            hn[2 * irow : 4 * irow, :], h[rows : 2 * rows, :]
        )
        first = far_first + per_step * order(step)
        for n in range(per_step):
            kt[first + n] = value[n * unit : (n + 1) * unit]
            share(first + n)
    for step in (NB - 2, NB - 1):
        each(far_first + per_step * order(step), per_step, chain)

    for k in range(C_CHUNKS):
        c_forward(k).wait_send()
    for step in range(NB):
        for p in range(2):
            i_across(step, p).wait_send()
            i_core(step, p, o).wait_send()
    each(side, side, finish)
    each(far_first, side, finish)


def pair_device(naux, integrals, coefficients, significant, domain):
    rows, band = integrals.shape[1:]
    occ = coefficients.shape[1]
    factor = 1.0 / math.sqrt(2 * naux * occ * 2)
    mine = band // (2 * naux)
    unit = 64
    chunks = band // unit
    dma = pltpu.SemaphoreType.DMA
    out = pl.pallas_call(
        functools.partial(pair_kernel, naux, rows, occ, factor),
        out_shape=jax.ShapeDtypeStruct((mine, rows), F32),
        in_specs=[
            pl.BlockSpec(memory_space=pltpu.SMEM),
            pl.BlockSpec(memory_space=pltpu.SMEM),
            pl.BlockSpec(memory_space=pl.ANY),
            pl.BlockSpec(memory_space=pl.ANY),
        ],
        out_specs=pl.BlockSpec(memory_space=pltpu.VMEM),
        scratch_shapes=[
            pltpu.VMEM((rows, occ), BF16),
            pltpu.VMEM((2 * rows, occ), BF16),
            pltpu.VMEM((2 * rows, 2 * rows), BF16),
            pltpu.VMEM((2 * rows, 2 * rows), BF16),
            pltpu.VMEM((2 * rows, occ), F32),
            pltpu.VMEM((2 * rows, occ), BF16),
            pltpu.VMEM((2 * rows // NB, occ), BF16),
            pltpu.VMEM((chunks, unit, rows), F32),
            pltpu.VMEM((chunks, unit, rows), F32),
            pltpu.VMEM((chunks, unit, rows), F32),
            pltpu.VMEM((chunks, unit, rows), F32),
            pltpu.VMEM((2, occ), F32),
            dma((3,)),
            dma((C_CHUNKS,)), dma((C_CHUNKS,)), dma((C_CHUNKS,)), dma((C_CHUNKS,)),
            dma((NB, 2)), dma((NB, 2)), dma((NB, 2)), dma((NB, 2)),
            dma((chunks,)), dma((chunks,)), dma((chunks,)),
            dma((chunks,)), dma((chunks,)), dma((chunks,)),
        ],
        compiler_params=pltpu.CompilerParams(
            collective_id=0, has_side_effects=True, vmem_limit_bytes=48 * 1024 * 1024
        ),
    )(significant, domain, integrals, coefficients)
    return out.T


def solution(mesh):
    placed = (
        P(("groups", "aux"), "ao", None),
        P(("groups", "ao"), "occ"),
        P(("groups", "ao"), "occ"),
        P(("groups", "aux"), "occ"),
    )
    two_groups = mesh.shape["ao"] == 2 and mesh.shape["aux"] == 4 and mesh.shape["occ"] == 2
    body = functools.partial(pair_device, mesh.shape["aux"]) if two_groups else per_device
    return jax.shard_map(
        body,
        mesh=mesh,
        in_specs=placed,
        out_specs=P(("groups", "ao"), ("aux", "occ")),
        check_vma=False,
    )
```

```python
import functools
import math

import jax
import jax.numpy as jnp
from jax import lax
from jax.experimental import pallas as pl
from jax.experimental.pallas import tpu as pltpu
from jax.sharding import PartitionSpec as P

TILE = 128
MESH = pl.DeviceIdType.MESH
F32 = jnp.float32
BF16 = jnp.bfloat16
C_CHUNKS = 8
NB = 4


def with_halo(block, sides, width):
    for axis, dim in sides:
        count = lax.axis_size(axis)
        forward = [(i, i + 1) for i in range(count - 1)]
        backward = [(target, source) for source, target in forward]
        low = lax.ppermute(
            lax.slice_in_dim(block, block.shape[dim] - width, None, axis=dim), axis, forward
        )
        high = lax.ppermute(lax.slice_in_dim(block, 0, width, axis=dim), axis, backward)
        block = jnp.concatenate([low, block, high], axis=dim)
    return block


def per_device(integrals, coefficients, significant, domain):
    slab_count = integrals.shape[0]
    row_count = integrals.shape[1]
    band_width = integrals.shape[2]
    occ_count = coefficients.shape[1]
    reach = (band_width - row_count) // 2
    expanded = jnp.repeat(jnp.repeat(significant, TILE, 0), TILE, 1)
    masked = coefficients * expanded.astype(jnp.bfloat16)
    window = with_halo(masked, (("ao", 0),), reach)
    flattened = integrals.reshape(slab_count * row_count, band_width)
    product = jnp.dot(flattened, window, preferred_element_type=jnp.float32)
    product = product.reshape(slab_count, row_count, occ_count)
    limits = jnp.repeat(domain[0], TILE)
    aux_place = jnp.arange(slab_count, dtype=jnp.int32)
    retain = (aux_place[:, None] < limits[None, :]).astype(jnp.float32)
    half_form = (product * retain[:, None, :]).astype(jnp.bfloat16)
    nearby = with_halo(half_form, (("ao", 1),), reach)
    aux_devices = lax.axis_size("aux")
    occ_devices = lax.axis_size("occ")
    factor = 1.0 / math.sqrt(slab_count * aux_devices * occ_count * occ_devices)
    exchange_term = (
        lax.dot_general(
            half_form, nearby, (((0, 2), (0, 2)), ((), ())), preferred_element_type=jnp.float32
        )
        * factor
    )
    return lax.psum_scatter(exchange_term, ("aux", "occ"), scatter_dimension=1, tiled=True)


def dot_nt(a, b):
    return lax.dot_general(a, b, (((1,), (1,)), ((), ())), preferred_element_type=F32)


def aligned(value, unit):
    return pl.multiple_of(value, unit)


def pair_kernel(
    naux, rows, occ, factor,
    sig_ref, dom_ref, int_ref, coef_ref, out_ref,
    craw, cw, iw, inb, acc, h, hn, kt, kc, rup, rdn, keep,
    load_sem, c_send, c_recv, f_send, f_recv, i_send, i_recv, g_send, g_recv,
    k_send, k_recv, up_send, up_recv, dn_send, dn_recv,
):
    z = lax.axis_index("aux")
    x = lax.axis_index("ao")
    o = lax.axis_index("occ")
    par = lax.rem(z, 2)
    partner = z + 1 - 2 * par
    unit = kt.shape[1]
    per_dev = out_ref.shape[0] // unit
    side = rows // unit
    crow = rows // 2 // C_CHUNKS
    irow = rows // NB // 2

    load_c = pltpu.make_async_copy(coef_ref, craw, load_sem.at[0])
    load_c.start()
    loads = []
    for p in range(2):
        load = pltpu.make_async_copy(
            int_ref.at[p, :, pl.ds(aligned((1 - x) * rows, rows), 2 * rows)],
            iw.at[pl.ds(p * rows, rows)],
            load_sem.at[1 + p],
        )
        load.start()
        loads.append(load)

    barrier = pltpu.get_barrier_semaphore()
    pl.semaphore_signal(barrier, inc=1, device_id={"ao": 1 - x}, device_id_type=MESH)
    pl.semaphore_signal(barrier, inc=1, device_id={"occ": 1 - o}, device_id_type=MESH)

    @pl.when(z > 0)
    def _():
        pl.semaphore_signal(barrier, inc=1, device_id={"aux": z - 1}, device_id_type=MESH)

    @pl.when(z < naux - 1)
    def _():
        pl.semaphore_signal(barrier, inc=1, device_id={"aux": z + 1}, device_id_type=MESH)

    block_of = lax.broadcasted_iota(jnp.int32, (1, occ), 1) // TILE

    def expand(ref, row):
        line = jnp.zeros((1, occ), F32)
        for j in range(occ // TILE):
            line = jnp.where(block_of == j, ref[row, j].astype(F32), line)
        return line

    limits = expand(dom_ref, 0)
    for p in range(2):
        keep[p : p + 1, :] = jnp.where(limits > float(p), 1.0, 0.0)
    load_c.wait()
    for b in range(rows // TILE):
        mask = expand(sig_ref, b).astype(BF16)
        cw[pl.ds(aligned(x * rows + b * TILE, TILE), TILE), :] = (
            craw[b * TILE : (b + 1) * TILE, :] * mask
        )

    @pl.when((z > 0) & (z < naux - 1))
    def _():
        pl.semaphore_wait(barrier, 4)

    @pl.when((z == 0) | (z == naux - 1))
    def _():
        pl.semaphore_wait(barrier, 3)

    def c_copy(k, owner, half, send, recv, target):
        part = cw.at[pl.ds(aligned(owner * rows + half * (rows // 2) + k * crow, crow), crow)]
        return pltpu.make_async_remote_copy(
            src_ref=part, dst_ref=part, send_sem=send.at[k], recv_sem=recv.at[k],
            device_id=target, device_id_type=MESH,
        )

    def c_across(k):
        return c_copy(k, x, par, c_send, c_recv, {"ao": 1 - x})

    def c_arrival(k):
        return c_copy(k, 1 - x, par, c_send, c_recv, {"ao": 1 - x})

    def c_forward(k):
        return c_copy(k, 1 - x, par, f_send, f_recv, {"aux": partner})

    def c_forwarded(k):
        return c_copy(k, 1 - x, 1 - par, f_send, f_recv, {"aux": partner})

    for k in range(C_CHUNKS):
        c_across(k).start()

    def order(step):
        return step + (NB - 1 - 2 * step) * (1 - x)

    def i_across(step, p):
        j = order_peer(step)
        return pltpu.make_async_remote_copy(
            src_ref=iw.at[pl.ds(aligned(p * rows + j * 2 * irow + o * irow, irow), irow)],
            dst_ref=inb.at[pl.ds(aligned(step * 4 * irow + p * 2 * irow + o * irow, irow), irow)],
            send_sem=i_send.at[step, p], recv_sem=i_recv.at[step, p],
            device_id={"ao": 1 - x}, device_id_type=MESH,
        )

    def order_peer(step):
        return step + (NB - 1 - 2 * step) * x

    def i_core(step, p, core):
        part = inb.at[pl.ds(aligned(step * 4 * irow + p * 2 * irow + core * irow, irow), irow)]
        return pltpu.make_async_remote_copy(
            src_ref=part, dst_ref=part, send_sem=g_send.at[step, p], recv_sem=g_recv.at[step, p],
            device_id={"occ": 1 - o}, device_id_type=MESH,
        )

    for load in loads:
        load.wait()

    width = 256
    own_rows = pl.ds(aligned(x * rows, rows), rows)
    far_rows = pl.ds(aligned((1 - x) * rows, rows), rows)

    def own_tile(t, carry):
        cols = pl.ds(aligned(t * width, width), width)
        acc[:, cols] = jnp.dot(iw[:, own_rows], cw[own_rows, cols], preferred_element_type=F32)
        return carry

    lax.fori_loop(0, occ // width, own_tile, 0)

    for k in range(C_CHUNKS):
        c_arrival(k).wait_recv()
        c_forward(k).start()
    for k in range(C_CHUNKS):
        c_across(k).wait_send()
    for step in range(NB):
        for p in range(2):
            i_across(step, p).start()
    for k in range(C_CHUNKS):
        c_forwarded(k).wait_recv()

    def far_tile(t, carry):
        cols = pl.ds(aligned(t * width, width), width)
        total = acc[:, cols] + jnp.dot(
            iw[:, far_rows], cw[far_rows, cols], preferred_element_type=F32
        )
        for p in range(2):
            h[p * rows : (p + 1) * rows, cols] = (
                total[p * rows : (p + 1) * rows] * keep[p : p + 1, cols]
            ).astype(BF16)
        return carry

    lax.fori_loop(0, occ // width, far_tile, 0)

    def core_copy(idx):
        return pltpu.make_async_remote_copy(
            src_ref=kt.at[idx], dst_ref=kc.at[idx], send_sem=k_send.at[idx],
            recv_sem=k_recv.at[idx], device_id={"occ": 1 - o}, device_id_type=MESH,
        )

    def up_copy(idx):
        return pltpu.make_async_remote_copy(
            src_ref=kt.at[idx], dst_ref=rup.at[idx], send_sem=up_send.at[idx],
            recv_sem=up_recv.at[idx], device_id={"aux": z + 1}, device_id_type=MESH,
        )

    def down_copy(idx):
        return pltpu.make_async_remote_copy(
            src_ref=kt.at[idx], dst_ref=rdn.at[idx], send_sem=dn_send.at[idx],
            recv_sem=dn_recv.at[idx], device_id={"aux": z - 1}, device_id_type=MESH,
        )

    def place(idx):
        owner = idx // per_dev
        return owner // 2, lax.rem(owner, 2), lax.rem(idx, per_dev)

    def share(idx):
        _, ot, _ = place(idx)

        @pl.when(ot != o)
        def _():
            core_copy(idx).start()

    def chain(idx):
        zt, ot, _ = place(idx)

        @pl.when((ot == o) & (z != zt))
        def _():
            core_copy(idx).wait_recv()
            kt[idx] = kt[idx] + kc[idx]

            @pl.when((z > 0) & (z < zt))
            def _():
                up_copy(idx).wait_recv()
                kt[idx] = kt[idx] + rup[idx]

            @pl.when((z < naux - 1) & (z > zt))
            def _():
                down_copy(idx).wait_recv()
                kt[idx] = kt[idx] + rdn[idx]

            @pl.when(z < zt)
            def _():
                up_copy(idx).start()

            @pl.when(z > zt)
            def _():
                down_copy(idx).start()

    def arrive(idx):
        zt, ot, s = place(idx)

        @pl.when((ot == o) & (z == zt))
        def _():
            core_copy(idx).wait_recv()
            kt[idx] = kt[idx] + kc[idx]

            @pl.when(z > 0)
            def _():
                up_copy(idx).wait_recv()
                kt[idx] = kt[idx] + rup[idx]

            @pl.when(z < naux - 1)
            def _():
                down_copy(idx).wait_recv()
                kt[idx] = kt[idx] + rdn[idx]

            out_ref[pl.ds(aligned(s * unit, unit), unit), :] = kt[idx] * factor

    def finish(idx):
        zt, ot, _ = place(idx)

        @pl.when(ot != o)
        def _():
            core_copy(idx).wait_send()

        @pl.when((ot == o) & (z < zt))
        def _():
            up_copy(idx).wait_send()

        @pl.when((ot == o) & (z > zt))
        def _():
            down_copy(idx).wait_send()

    def each(first, count, body):
        def step(n, carry):
            body(first + n)
            return carry

        lax.fori_loop(0, count, step, 0)

    out_ref[...] = jnp.zeros_like(out_ref)

    flip = jnp.where(z < naux // 2, 1, 0)

    def own_block(n, carry):
        t = n + flip * (side // 2 - 1 - 2 * n)
        base = aligned(t * 2 * unit, 2 * unit)
        value = dot_nt(h[pl.ds(base, 2 * unit), :], h[0:rows, :]) + dot_nt(
            h[pl.ds(aligned(rows + base, 2 * unit), 2 * unit), :], h[rows : 2 * rows, :]
        )
        kt[side + 2 * t] = value[:unit]
        kt[side + 2 * t + 1] = value[unit:]
        share(side + 2 * t)
        share(side + 2 * t + 1)
        return carry

    lax.fori_loop(0, side // 2, own_block, 0)

    def own_chain(n, carry):
        chain(side + n + flip * (side - 1 - 2 * n))
        return carry

    def end_chain():
        lax.fori_loop(0, side, own_chain, 0)

    @pl.when((z == 0) | (z == naux - 1))
    def _():
        end_chain()

    far_first = 2 * side * (1 - x)
    per_step = side // NB
    for step in range(NB):
        for p in range(2):
            i_across(step, p).wait_recv()
            i_core(step, p, o).start()
        for p in range(2):
            i_core(step, p, 1 - o).wait_recv()
        base = step * 4 * irow

        def near_tile(t, carry):
            cols = pl.ds(aligned(t * width, width), width)
            total = jnp.dot(
                inb[base : base + 4 * irow, :], cw[:, cols], preferred_element_type=F32
            )
            for p in range(2):
                hn[p * 2 * irow : (p + 1) * 2 * irow, cols] = (
                    total[p * 2 * irow : (p + 1) * 2 * irow] * keep[p : p + 1, cols]
                ).astype(BF16)
            return carry

        lax.fori_loop(0, occ // width, near_tile, 0)
        value = dot_nt(hn[0 : 2 * irow, :], h[0:rows, :]) + dot_nt(
            hn[2 * irow : 4 * irow, :], h[rows : 2 * rows, :]
        )
        first = far_first + per_step * order(step)
        for n in range(per_step):
            kt[first + n] = value[n * unit : (n + 1) * unit]
            share(first + n)
        if step == 0:

            @pl.when((z > 0) & (z < naux - 1))
            def _():
                end_chain()

        each(first, per_step, chain)
    each(side, side, arrive)
    for step in range(NB):
        each(far_first + per_step * order(step), per_step, arrive)

    for k in range(C_CHUNKS):
        c_forward(k).wait_send()
    for step in range(NB):
        for p in range(2):
            i_across(step, p).wait_send()
            i_core(step, p, o).wait_send()
    each(side, side, finish)
    each(far_first, side, finish)


def pair_device(naux, integrals, coefficients, significant, domain):
    rows, band = integrals.shape[1:]
    occ = coefficients.shape[1]
    factor = 1.0 / math.sqrt(2 * naux * occ * 2)
    mine = band // (2 * naux)
    unit = 64
    chunks = band // unit
    dma = pltpu.SemaphoreType.DMA
    out = pl.pallas_call(
        functools.partial(pair_kernel, naux, rows, occ, factor),
        out_shape=jax.ShapeDtypeStruct((mine, rows), F32),
        in_specs=[
            pl.BlockSpec(memory_space=pltpu.SMEM),
            pl.BlockSpec(memory_space=pltpu.SMEM),
            pl.BlockSpec(memory_space=pltpu.HBM),
            pl.BlockSpec(memory_space=pltpu.HBM),
        ],
        out_specs=pl.BlockSpec(memory_space=pltpu.VMEM),
        scratch_shapes=[
            pltpu.VMEM((rows, occ), BF16),
            pltpu.VMEM((2 * rows, occ), BF16),
            pltpu.VMEM((2 * rows, 2 * rows), BF16),
            pltpu.VMEM((2 * rows, 2 * rows), BF16),
            pltpu.VMEM((2 * rows, occ), F32),
            pltpu.VMEM((2 * rows, occ), BF16),
            pltpu.VMEM((2 * rows // NB, occ), BF16),
            pltpu.VMEM((chunks, unit, rows), F32),
            pltpu.VMEM((chunks, unit, rows), F32),
            pltpu.VMEM((chunks, unit, rows), F32),
            pltpu.VMEM((chunks, unit, rows), F32),
            pltpu.VMEM((2, occ), F32),
            dma((3,)),
            dma((C_CHUNKS,)), dma((C_CHUNKS,)), dma((C_CHUNKS,)), dma((C_CHUNKS,)),
            dma((NB, 2)), dma((NB, 2)), dma((NB, 2)), dma((NB, 2)),
            dma((chunks,)), dma((chunks,)), dma((chunks,)),
            dma((chunks,)), dma((chunks,)), dma((chunks,)),
        ],
        compiler_params=pltpu.CompilerParams(
            collective_id=0, has_side_effects=True, vmem_limit_bytes=60 * 1024 * 1024
        ),
    )(significant, domain, integrals, coefficients)
    return out.T


def solution(mesh):
    placed = (
        P(("groups", "aux"), "ao", None),
        P(("groups", "ao"), "occ"),
        P(("groups", "ao"), "occ"),
        P(("groups", "aux"), "occ"),
    )
    two_groups = mesh.shape["ao"] == 2 and mesh.shape["aux"] == 4 and mesh.shape["occ"] == 2
    body = functools.partial(pair_device, mesh.shape["aux"]) if two_groups else per_device
    return jax.shard_map(
        body,
        mesh=mesh,
        in_specs=placed,
        out_specs=P(("groups", "ao"), ("aux", "occ")),
        check_vma=False,
    )
```

```python
import functools
import math

import jax
import jax.numpy as jnp
from jax import lax
from jax.experimental import pallas as pl
from jax.experimental.pallas import tpu as pltpu
from jax.sharding import PartitionSpec as P

TILE = 128
MESH = pl.DeviceIdType.MESH
F32 = jnp.float32
BF16 = jnp.bfloat16
C_CHUNKS = 8
NB = 4


def with_halo(block, sides, width):
    for axis, dim in sides:
        count = lax.axis_size(axis)
        forward = [(i, i + 1) for i in range(count - 1)]
        backward = [(target, source) for source, target in forward]
        low = lax.ppermute(
            lax.slice_in_dim(block, block.shape[dim] - width, None, axis=dim), axis, forward
        )
        high = lax.ppermute(lax.slice_in_dim(block, 0, width, axis=dim), axis, backward)
        block = jnp.concatenate([low, block, high], axis=dim)
    return block


def per_device(integrals, coefficients, significant, domain):
    slab_count = integrals.shape[0]
    row_count = integrals.shape[1]
    band_width = integrals.shape[2]
    occ_count = coefficients.shape[1]
    reach = (band_width - row_count) // 2
    expanded = jnp.repeat(jnp.repeat(significant, TILE, 0), TILE, 1)
    masked = coefficients * expanded.astype(jnp.bfloat16)
    window = with_halo(masked, (("ao", 0),), reach)
    flattened = integrals.reshape(slab_count * row_count, band_width)
    product = jnp.dot(flattened, window, preferred_element_type=jnp.float32)
    product = product.reshape(slab_count, row_count, occ_count)
    limits = jnp.repeat(domain[0], TILE)
    aux_place = jnp.arange(slab_count, dtype=jnp.int32)
    retain = (aux_place[:, None] < limits[None, :]).astype(jnp.float32)
    half_form = (product * retain[:, None, :]).astype(jnp.bfloat16)
    nearby = with_halo(half_form, (("ao", 1),), reach)
    aux_devices = lax.axis_size("aux")
    occ_devices = lax.axis_size("occ")
    factor = 1.0 / math.sqrt(slab_count * aux_devices * occ_count * occ_devices)
    exchange_term = (
        lax.dot_general(
            half_form, nearby, (((0, 2), (0, 2)), ((), ())), preferred_element_type=jnp.float32
        )
        * factor
    )
    return lax.psum_scatter(exchange_term, ("aux", "occ"), scatter_dimension=1, tiled=True)


def aligned(value, unit):
    return pl.multiple_of(value, unit)


def pair_kernel(
    naux, rows, occ, factor,
    sig_ref, dom_ref, int_ref, coef_ref, out_ref,
    craw, cw, iw, inb, acc, ht, hn, kown, kt, kc, rup, rdn, kb, rb, keep, masks,
    load_sem, m_send, m_recv, c_send, c_recv, f_send, f_recv, i_send, i_recv, g_send, g_recv,
    ld_send, ld_recv, k_send, k_recv, up_send, up_recv, dn_send, dn_recv,
):
    z = lax.axis_index("aux")
    x = lax.axis_index("ao")
    o = lax.axis_index("occ")
    par = lax.rem(z, 2)
    partner = z + 1 - 2 * par
    unit = kt.shape[1]
    per_dev = out_ref.shape[0] // unit
    side = rows // unit
    irow = rows // NB // 2
    width = occ // C_CHUNKS
    own_rows = pl.ds(aligned(x * rows, rows), rows)
    far_rows = pl.ds(aligned((1 - x) * rows, rows), rows)
    near_cols = pl.ds(aligned((1 - x) * rows, rows), 2 * rows)

    load_c = pltpu.make_async_copy(coef_ref, craw.at[own_rows], load_sem.at[0])
    load_c.start()
    loads = []
    for p in range(2):
        load = pltpu.make_async_copy(
            int_ref.at[p, :, near_cols], iw.at[pl.ds(p * rows, rows)], load_sem.at[1 + p]
        )
        load.start()
        loads.append(load)

    barrier = pltpu.get_barrier_semaphore()
    pl.semaphore_signal(barrier, inc=1, device_id={"ao": 1 - x}, device_id_type=MESH)
    pl.semaphore_signal(barrier, inc=1, device_id={"occ": 1 - o}, device_id_type=MESH)

    @pl.when(z > 0)
    def _():
        pl.semaphore_signal(barrier, inc=1, device_id={"aux": z - 1}, device_id_type=MESH)

    @pl.when(z < naux - 1)
    def _():
        pl.semaphore_signal(barrier, inc=1, device_id={"aux": z + 1}, device_id_type=MESH)

    block_of = lax.broadcasted_iota(jnp.int32, (1, occ), 1) // TILE

    def expand(ref, row):
        line = jnp.zeros((1, occ), F32)
        for j in range(occ // TILE):
            line = jnp.where(block_of == j, ref[row, j].astype(F32), line)
        return line

    blocks = rows // TILE
    masks[x] = jnp.concatenate(
        [expand(sig_ref, b) for b in range(blocks)] + [jnp.zeros((8 - blocks, occ), F32)], 0
    )

    @pl.when((z > 0) & (z < naux - 1))
    def _():
        pl.semaphore_wait(barrier, 4)

    @pl.when((z == 0) | (z == naux - 1))
    def _():
        pl.semaphore_wait(barrier, 3)

    def mask_copy(owner):
        return pltpu.make_async_remote_copy(
            src_ref=masks.at[owner], dst_ref=masks.at[owner], send_sem=m_send, recv_sem=m_recv,
            device_id={"ao": 1 - x}, device_id_type=MESH,
        )

    def c_region(owner, half, k):
        return craw.at[
            pl.ds(aligned(owner * rows + half * (rows // 2), rows // 2), rows // 2),
            pl.ds(k * width, width),
        ]

    def c_across(k):
        return pltpu.make_async_remote_copy(
            src_ref=coef_ref.at[
                pl.ds(aligned(par * (rows // 2), rows // 2), rows // 2), pl.ds(k * width, width)
            ],
            dst_ref=c_region(x, par, k), send_sem=c_send.at[k], recv_sem=c_recv.at[k],
            device_id={"ao": 1 - x}, device_id_type=MESH,
        )

    def c_arrival(k):
        part = c_region(1 - x, par, k)
        return pltpu.make_async_remote_copy(
            src_ref=part, dst_ref=part, send_sem=c_send.at[k], recv_sem=c_recv.at[k],
            device_id={"ao": 1 - x}, device_id_type=MESH,
        )

    def c_forward(k, half):
        part = c_region(1 - x, half, k)
        return pltpu.make_async_remote_copy(
            src_ref=part, dst_ref=part, send_sem=f_send.at[k], recv_sem=f_recv.at[k],
            device_id={"aux": partner}, device_id_type=MESH,
        )

    mask_copy(x).start()
    for k in range(C_CHUNKS):
        c_across(k).start()

    def order(step):
        return step + (NB - 1 - 2 * step) * (1 - x)

    def order_peer(step):
        return step + (NB - 1 - 2 * step) * x

    def i_across(step, p):
        j = order_peer(step)
        return pltpu.make_async_remote_copy(
            src_ref=int_ref.at[p, pl.ds(aligned(j * 2 * irow + o * irow, irow), irow), near_cols],
            dst_ref=inb.at[pl.ds(aligned(step * 4 * irow + p * 2 * irow + o * irow, irow), irow)],
            send_sem=i_send.at[step, p], recv_sem=i_recv.at[step, p],
            device_id={"ao": 1 - x}, device_id_type=MESH,
        )

    def i_core(step, p, core):
        part = inb.at[pl.ds(aligned(step * 4 * irow + p * 2 * irow + core * irow, irow), irow)]
        return pltpu.make_async_remote_copy(
            src_ref=part, dst_ref=part, send_sem=g_send.at[step, p], recv_sem=g_recv.at[step, p],
            device_id={"occ": 1 - o}, device_id_type=MESH,
        )

    def i_begin(step):
        for p in range(2):
            i_across(step, p).start()

    out_ref[...] = jnp.zeros_like(out_ref)
    limits = expand(dom_ref, 0)
    for p in range(2):
        keep[p : p + 1, :] = jnp.where(limits > float(p), 1.0, 0.0)

    def mask_rows(owner, cols):
        for b in range(blocks):
            part = pl.ds(aligned(owner * rows + b * TILE, TILE), TILE)
            cw[part, cols] = craw[part, cols] * masks[owner, b : b + 1, cols].astype(BF16)

    load_c.wait()
    mask_rows(x, pl.ds(0, occ))
    for load in loads:
        load.wait()
    tile = 256

    def own_tile(t, carry):
        cols = pl.ds(aligned(t * tile, tile), tile)
        acc[:, cols] = jnp.dot(iw[:, own_rows], cw[own_rows, cols], preferred_element_type=F32)
        return carry

    lax.fori_loop(0, occ // tile, own_tile, 0)
    mask_copy(1 - x).wait_recv()
    kown[...] = jnp.zeros_like(kown)

    def far_tile(k, carry):
        cols = pl.ds(aligned(k * tile, tile), tile)
        mask_rows(1 - x, cols)
        total = acc[:, cols] + jnp.dot(
            iw[:, far_rows], cw[far_rows, cols], preferred_element_type=F32
        )
        for p in range(2):
            part = (total[p * rows : (p + 1) * rows] * keep[p : p + 1, cols]).astype(BF16)
            turned = part.T
            ht[p, cols, :] = turned
            kown[...] += jnp.dot(part, turned, preferred_element_type=F32)
        return carry

    pieces = tile // width
    for k in range(C_CHUNKS):
        c_arrival(k).wait_recv()
        c_forward(k, par).start()
        if k == C_CHUNKS - 2:
            i_begin(0)
        if k % pieces == pieces - 1 and k >= 2 * pieces - 1:
            t = k // pieces - 1
            for n in range(pieces):
                c_forward(t * pieces + n, 1 - par).wait_recv()
            far_tile(t, 0)
    i_begin(1)
    for n in range(pieces):
        c_forward(C_CHUNKS - pieces + n, 1 - par).wait_recv()
    far_tile(occ // tile - 1, 0)

    def core_copy(idx):
        return pltpu.make_async_remote_copy(
            src_ref=kt.at[idx], dst_ref=kc.at[idx], send_sem=k_send.at[idx],
            recv_sem=k_recv.at[idx], device_id={"occ": 1 - o}, device_id_type=MESH,
        )

    def up_copy(idx):
        return pltpu.make_async_remote_copy(
            src_ref=kt.at[idx], dst_ref=rup.at[idx], send_sem=up_send.at[idx],
            recv_sem=up_recv.at[idx], device_id={"aux": z + 1}, device_id_type=MESH,
        )

    def down_copy(idx):
        return pltpu.make_async_remote_copy(
            src_ref=kt.at[idx], dst_ref=rdn.at[idx], send_sem=dn_send.at[idx],
            recv_sem=dn_recv.at[idx], device_id={"aux": z - 1}, device_id_type=MESH,
        )

    def place(idx):
        owner = idx // per_dev
        return owner // 2, lax.rem(owner, 2), lax.rem(idx, per_dev)

    def share(idx):
        _, ot, _ = place(idx)

        @pl.when(ot != o)
        def _():
            core_copy(idx).start()

    lead = jnp.where(x == 0, 0, naux - 1)
    second = jnp.where(x == 0, 1, naux - 2)
    inward = 1 - 2 * x

    def lead_copy(idx):
        return pltpu.make_async_remote_copy(
            src_ref=kb.at[idx], dst_ref=rb.at[idx], send_sem=ld_send.at[idx],
            recv_sem=ld_recv.at[idx], device_id={"aux": z + inward}, device_id_type=MESH,
        )

    def lead_landed(idx):
        return pltpu.make_async_remote_copy(
            src_ref=kb.at[idx], dst_ref=rb.at[idx], send_sem=ld_send.at[idx],
            recv_sem=ld_recv.at[idx], device_id={"aux": z - inward}, device_id_type=MESH,
        )

    def gather(idx, zt):
        core_copy(idx).wait_recv()
        kt[idx] = kt[idx] + kc[idx]

        @pl.when((z > 0) & (z <= zt) & ((x == 1) | (z != second)))
        def _():
            up_copy(idx).wait_recv()
            kt[idx] = kt[idx] + rup[idx]

        @pl.when((z < naux - 1) & (z >= zt) & ((x == 0) | (z != second)))
        def _():
            down_copy(idx).wait_recv()
            kt[idx] = kt[idx] + rdn[idx]

        @pl.when((z == second) & (((x == 0) & (zt >= second)) | ((x == 1) & (zt <= second))))
        def _():
            lead_landed(idx).wait_recv()
            kt[idx] = kt[idx] + rb[idx].astype(F32)

    def chain(idx):
        zt, ot, _ = place(idx)

        @pl.when((ot == o) & (z != zt))
        def _():
            gather(idx, zt)

            @pl.when(z == lead)
            def _():
                kb[idx] = kt[idx].astype(BF16)
                lead_copy(idx).start()

            @pl.when((z < zt) & (z != lead))
            def _():
                up_copy(idx).start()

            @pl.when((z > zt) & (z != lead))
            def _():
                down_copy(idx).start()

    def arrive(idx):
        zt, ot, s = place(idx)

        @pl.when((ot == o) & (z == zt))
        def _():
            gather(idx, zt)
            out_ref[pl.ds(aligned(s * unit, unit), unit), :] = kt[idx] * factor

    def finish(idx):
        zt, ot, _ = place(idx)

        @pl.when(ot != o)
        def _():
            core_copy(idx).wait_send()

        @pl.when((ot == o) & (z != zt) & (z == lead))
        def _():
            lead_copy(idx).wait_send()

        @pl.when((ot == o) & (z < zt) & (z != lead))
        def _():
            up_copy(idx).wait_send()

        @pl.when((ot == o) & (z > zt) & (z != lead))
        def _():
            down_copy(idx).wait_send()

    def each(first, count, body):
        def step(n, carry):
            body(first + n)
            return carry

        lax.fori_loop(0, count, step, 0)

    out_ref[...] = jnp.zeros_like(out_ref)

    flip = jnp.where(z < naux // 2, 1, 0)

    def own_block(n, carry):
        t = n + flip * (side - 1 - 2 * n)
        kt[side + t] = kown[pl.ds(aligned(t * unit, unit), unit), :]
        share(side + t)
        return carry

    lax.fori_loop(0, side, own_block, 0)

    def own_chain(n, carry):
        chain(side + n + flip * (side - 1 - 2 * n))
        return carry

    def end_chain():
        lax.fori_loop(0, side, own_chain, 0)

    @pl.when((z == 0) | (z == naux - 1))
    def _():
        end_chain()

    far_first = 2 * side * (1 - x)
    per_step = side // NB
    for step in range(NB):
        for p in range(2):
            i_across(step, p).wait_recv()
            i_core(step, p, o).start()
        if step + 2 < NB:
            i_begin(step + 2)
        for p in range(2):
            i_core(step, p, 1 - o).wait_recv()
        base = step * 4 * irow

        def near_tile(t, carry):
            cols = pl.ds(aligned(t * tile, tile), tile)
            total = jnp.dot(
                inb[base : base + 4 * irow, :], cw[:, cols], preferred_element_type=F32
            )
            for p in range(2):
                hn[p * 2 * irow : (p + 1) * 2 * irow, cols] = (
                    total[p * 2 * irow : (p + 1) * 2 * irow] * keep[p : p + 1, cols]
                ).astype(BF16)
            return carry

        lax.fori_loop(0, occ // tile, near_tile, 0)
        value = jnp.dot(hn[0 : 2 * irow, :], ht[0], preferred_element_type=F32) + jnp.dot(
            hn[2 * irow : 4 * irow, :], ht[1], preferred_element_type=F32
        )
        first = far_first + per_step * order(step)
        for n in range(per_step):
            kt[first + n] = value[n * unit : (n + 1) * unit]
            share(first + n)
        if step == 0:

            @pl.when((z > 0) & (z < naux - 1))
            def _():
                end_chain()

        each(first, per_step, chain)
    each(side, side, arrive)
    for step in range(NB):
        each(far_first + per_step * order(step), per_step, arrive)

    mask_copy(x).wait_send()
    for k in range(C_CHUNKS):
        c_across(k).wait_send()
        c_forward(k, par).wait_send()
    for step in range(NB):
        for p in range(2):
            i_across(step, p).wait_send()
            i_core(step, p, o).wait_send()
    each(side, side, finish)
    each(far_first, side, finish)


def pair_device(naux, integrals, coefficients, significant, domain):
    rows, band = integrals.shape[1:]
    occ = coefficients.shape[1]
    factor = 1.0 / math.sqrt(2 * naux * occ * 2)
    mine = band // (2 * naux)
    unit = 64
    chunks = band // unit
    dma = pltpu.SemaphoreType.DMA
    out = pl.pallas_call(
        functools.partial(pair_kernel, naux, rows, occ, factor),
        out_shape=jax.ShapeDtypeStruct((mine, rows), F32),
        in_specs=[
            pl.BlockSpec(memory_space=pltpu.SMEM),
            pl.BlockSpec(memory_space=pltpu.SMEM),
            pl.BlockSpec(memory_space=pltpu.HBM),
            pl.BlockSpec(memory_space=pltpu.HBM),
        ],
        out_specs=pl.BlockSpec(memory_space=pltpu.VMEM),
        scratch_shapes=[
            pltpu.VMEM((2 * rows, occ), BF16),
            pltpu.VMEM((2 * rows, occ), BF16),
            pltpu.VMEM((2 * rows, 2 * rows), BF16),
            pltpu.VMEM((2 * rows, 2 * rows), BF16),
            pltpu.VMEM((2 * rows, occ), F32),
            pltpu.VMEM((2, occ, rows), BF16),
            pltpu.VMEM((2 * rows // NB, occ), BF16),
            pltpu.VMEM((rows, rows), F32),
            pltpu.VMEM((chunks, unit, rows), F32),
            pltpu.VMEM((chunks, unit, rows), F32),
            pltpu.VMEM((chunks, unit, rows), F32),
            pltpu.VMEM((chunks, unit, rows), F32),
            pltpu.VMEM((chunks, unit, rows), BF16),
            pltpu.VMEM((chunks, unit, rows), BF16),
            pltpu.VMEM((2, occ), F32),
            pltpu.VMEM((2, 8, occ), F32),
            dma((3,)), dma, dma,
            dma((C_CHUNKS,)), dma((C_CHUNKS,)), dma((C_CHUNKS,)), dma((C_CHUNKS,)),
            dma((NB, 2)), dma((NB, 2)), dma((NB, 2)), dma((NB, 2)),
            dma((chunks,)), dma((chunks,)),
            dma((chunks,)), dma((chunks,)), dma((chunks,)),
            dma((chunks,)), dma((chunks,)), dma((chunks,)),
        ],
        compiler_params=pltpu.CompilerParams(
            collective_id=0, has_side_effects=True, vmem_limit_bytes=60 * 1024 * 1024
        ),
    )(significant, domain, integrals, coefficients)
    return out.T


def solution(mesh):
    placed = (
        P(("groups", "aux"), "ao", None),
        P(("groups", "ao"), "occ"),
        P(("groups", "ao"), "occ"),
        P(("groups", "aux"), "occ"),
    )
    two_groups = mesh.shape["ao"] == 2 and mesh.shape["aux"] == 4 and mesh.shape["occ"] == 2
    body = functools.partial(pair_device, mesh.shape["aux"]) if two_groups else per_device
    return jax.shard_map(
        body,
        mesh=mesh,
        in_specs=placed,
        out_specs=P(("groups", "ao"), ("aux", "occ")),
        check_vma=False,
    )
```
